32 devices in a mesh: seg: 4 (over z), tp: 4 (over y, core), dp: 2 (over x).
Axes of the slice: x: 2, y: 2, z: 4, core: 2. Of those that a mesh axis runs over, the one named last changes fastest.
Arguments:
- tokens: bfloat16 [8192, 4096], P(('dp', 'seg')), parts along dimension 0, may hold values from -64 to 64
- w_query: bfloat16 [4096, 2048], P(None, 'tp'), may hold values from -1 to 1
- w_key: bfloat16 [4096, 2048], P(None, 'tp'), may hold values from -1 to 1
- w_value: bfloat16 [4096, 2048], P(None, 'tp'), may hold values from -0.09375 to 0.09375
- w_out: bfloat16 [2048, 4096], P('tp'), may hold values from -1 to 1
- mem_gate: float32 [16], P('tp'), may hold values from -2 to 2
- resets: int32 [8], P(('dp', 'seg')), parts along dimension 0, may hold values 0 or 1
Outputs:
- layer_out: bfloat16 [8192, 4096], P(('dp', 'seg'), 'tp'), parts along dimension 0
The draws below stay inside these ranges and needn't reach their ends.
There are 2 independent parts, one for each index of `dp`. The reference program is written for one: setup_inputs(seed, part) draws one part's arguments, and reference() takes and returns one part's arrays. A program takes and returns all parts, laid end to end along the dimension named above; an argument that names none is the same for every part. Nothing has to cross between parts.
All inputs are finite; a program needn't handle non-finite values. No bound on the sum of `resets` on one device may be relied on, other than what follows from the above.
Results may differ from the reference program's by a relative error of at most 0.014.
Values may be sent and summed in bfloat16 or wider, within the bound.
A program may use at most 128 MiB of HBM per device.

```python
import math
import jax
import jax.numpy as jnp
from jax import lax

D = 4096
HEADS = 16
DH = 128
SEG_LEN = 1024
SEQ = 4096
N_SEG = 4
N_TP = 4


def draw_tokens(key, part):
    key_rows = jax.random.fold_in(key, 21)
    key_base = jax.random.fold_in(key, 22)
    row_scale = jnp.exp(jax.random.uniform(key_rows, (SEQ, 1), jnp.float32, math.log(0.3), math.log(3.0)))
    result = jnp.clip(jax.random.normal(key_base, (SEQ, D), jnp.float32), -4.0, 4.0) * row_scale
    return result.astype(jnp.bfloat16)


def shared_query(key):
    raw = jnp.clip(jax.random.normal(jax.random.fold_in(key, 11), (D, HEADS * DH), jnp.float32), -6.0, 6.0)
    return raw * (0.5 / math.sqrt(D))


def draw_w_query(key, part):
    return shared_query(key).astype(jnp.bfloat16)


def draw_w_key(key, part):
    other = jnp.clip(jax.random.normal(jax.random.fold_in(key, 12), (D, HEADS * DH), jnp.float32), -6.0, 6.0) * (0.5 / math.sqrt(D))
    result = other
    return result.astype(jnp.bfloat16)


def place_ends(drawn, own_key, low, top_value):
    index_at = [jax.random.randint(jax.random.fold_in(own_key, axis), (), 0, length) for axis, length in enumerate(drawn.shape)]
    longest = drawn.shape.index(max(drawn.shape))
    next_to = index_at[:longest] + [(index_at[longest] + 1) % drawn.shape[longest]] + index_at[longest + 1:]
    return drawn.at[tuple(index_at)].set(low).at[tuple(next_to)].set(top_value)


def block_scale(rng, dims, cuts, low, high):
    gain = 1.0
    for axis_at, blocks in cuts:
        steps = jax.random.uniform(jax.random.fold_in(jax.random.fold_in(rng, 6), axis_at), (blocks,), jnp.float32, low / len(cuts), high / len(cuts))
        gain = gain * jnp.repeat(jnp.exp(steps), dims[axis_at] // blocks).reshape((-1,) + (1,) * (len(dims) - 1 - axis_at))
    return gain


def gaussian(own_key, extent, deviation, limit, split=(), kind=jnp.bfloat16):
    factor_of = block_scale(own_key, extent, split, -0.22, 0.18) if split else 1.0
    drawn = jax.random.normal(own_key, extent, jnp.float32) * deviation * factor_of
    return jnp.minimum(jnp.maximum(drawn, -limit), limit).astype(kind)


def setup_inputs(seed: int = 0, part: int = 0) -> dict:
    key_of = jax.random.split(jax.random.key(seed), 8)
    own_keys = jax.random.split(jax.random.fold_in(key_of[7], part), 8)
    return {
        "tokens": draw_tokens(jax.random.fold_in(jax.random.fold_in(key_of[7], part), 71), part),
        "w_query": draw_w_query(jax.random.fold_in(key_of[7], 71), part),
        "w_key": draw_w_key(jax.random.fold_in(key_of[7], 71), part),
        "w_value": gaussian(key_of[3], (D, HEADS * DH), D ** -0.5, 0.09375, ((1, 4),)),
        "w_out": gaussian(key_of[4], (HEADS * DH, D), (HEADS * DH // 64) ** -0.5, 1.0, ((0, 4),)),
        "mem_gate": jnp.clip(jax.random.uniform(key_of[5], (HEADS,), jnp.float32, -2.0, 2.0) * block_scale(key_of[5], (HEADS,), ((0, 4),), -0.4, 0.0), -2.0, 2.0),
        "resets": place_ends((jax.random.randint(own_keys[6], (N_SEG,), 0, 5) < 1).astype(jnp.int32), jax.random.fold_in(own_keys[6], 1), 0, 1),
    }


def features(field):
    return jnp.where(field > 0, field + 1.0, jnp.exp(jnp.minimum(field, 0.0)))

def reference(tokens, w_query, w_key, w_value, w_out, mem_gate, resets):

    def project(weight):
        whole = jnp.dot(tokens, weight, preferred_element_type=jnp.float32).astype(jnp.bfloat16)
        return whole.reshape(N_SEG, SEG_LEN, HEADS, DH)
    queries = project(w_query)
    keys_all = project(w_key)
    vals_all = project(w_value)
    query_feat = features(queries.astype(jnp.float32))
    key_feat = features(keys_all.astype(jnp.float32))
    delta_mem = jnp.einsum('sthd,sthe->shde', key_feat, vals_all.astype(jnp.float32), precision=lax.Precision.HIGHEST)
    delta_norm = lax.optimization_barrier(jnp.sum(key_feat, axis=1))
    keep = 1.0 - resets.astype(jnp.float32)

    def advance(carry, item):
        memory, normer = carry
        keep_one, dmem, dnorm = item
        read_mem = keep_one * memory
        read_norm = keep_one * normer
        return ((read_mem + dmem, read_norm + dnorm), (read_mem, read_norm))
    start_state = (jnp.zeros((HEADS, DH, DH), jnp.float32), jnp.zeros((HEADS, DH), jnp.float32))
    _, (read_mem, read_norm) = lax.scan(advance, start_state, (keep, delta_mem, delta_norm))
    numer = jnp.einsum('sthd,shde->sthe', query_feat, read_mem, precision=lax.Precision.HIGHEST)
    denom = jnp.maximum(jnp.einsum('sthd,shd->sth', query_feat, read_norm, precision=lax.Precision.HIGHEST), 1.0)
    mem_att = numer / denom[..., None]

    def local_block(block):
        block_q, block_k, block_v = block
        scores = jnp.einsum('thd,uhd->htu', block_q.astype(jnp.float32), block_k.astype(jnp.float32), precision=lax.Precision.HIGHEST) / math.sqrt(DH)
        rows_idx = lax.broadcasted_iota(jnp.int32, (SEG_LEN, SEG_LEN), 0)
        cols_idx = lax.broadcasted_iota(jnp.int32, (SEG_LEN, SEG_LEN), 1)
        scores = jnp.where((rows_idx >= cols_idx)[None], scores, -1e+30)
        peak = lax.optimization_barrier(jnp.max(scores, axis=-1, keepdims=True))
        expo = jnp.exp(scores - peak)
        probs = (expo / lax.optimization_barrier(jnp.sum(expo, axis=-1, keepdims=True))).astype(jnp.bfloat16)
        return jnp.einsum('htu,uhd->thd', probs.astype(jnp.float32), block_v.astype(jnp.float32), precision=lax.Precision.HIGHEST)
    local_att = lax.map(local_block, (queries, keys_all, vals_all))
    gate = jax.nn.sigmoid(mem_gate)[None, None, :, None]
    attn = (gate * mem_att + (1.0 - gate) * local_att).astype(jnp.bfloat16).reshape(SEQ, HEADS * DH)
    group_cols = HEADS * DH // N_TP

    def add_group(total, group):
        start = (group * group_cols).astype(jnp.int32)
        cols = lax.dynamic_slice_in_dim(attn, start, group_cols, 1)
        rows = lax.dynamic_slice_in_dim(w_out, start, group_cols, 0)
        partial_value = jnp.dot(cols, rows, preferred_element_type=jnp.float32).astype(jnp.bfloat16)
        partial_value = lax.optimization_barrier(partial_value)
        return (total + partial_value.astype(jnp.float32), None)
    total, _ = lax.scan(add_group, jnp.zeros((SEQ, D), jnp.float32), jnp.arange(N_TP, dtype=jnp.int32))
    return total.astype(jnp.bfloat16)
```

```python
import functools
import math

import jax
import jax.numpy as jnp
from jax import lax
from jax.experimental import pallas as pl
from jax.experimental.pallas import tpu as pltpu
from jax.sharding import PartitionSpec as P

DH = 128
GW = 2 * DH
RB = 256
MB = 512
MESH = pl.DeviceIdType.MESH
F32 = jnp.float32
BF = jnp.bfloat16
SCALE = math.log2(math.e) / math.sqrt(DH)


def features(field):
    return jnp.where(field > 0, field + 1.0, jnp.exp(jnp.minimum(field, 0.0)))


def contract(a, b, dims):
    return lax.dot_general(a, b, (dims, ((), ())), preferred_element_type=F32)


def kernel(
    n_seg, n_tp, n_dp, sb,
    tok_hbm, wq_hbm, wk_hbm, wv_hbm, wo_hbm, gate_ref, keep_ref,
    out_hbm,
    tok, w, wo, q, k, v, kf, mem_out, mem_in, read, attn, acc, out,
    tok_sem, w_sem, own_sem, out_sem,
    wy_send, wy_recv, right_send, left_send, dp_send, shard_recv,
    mem_send, mem_recv, at_send, at_recv, fw_send,
):
    seg = lax.axis_index("seg")
    tp = lax.axis_index("tp")
    dp = lax.axis_index("dp")
    ny = n_tp // 2
    y, core = tp // 2, tp % 2
    rows = tok.shape[0]
    groups = q.shape[0]
    blocks = rows // RB
    out_cols = out.shape[1]
    depth = wo.shape[1] * wo.shape[2]
    pos = seg % sb
    sibling = y * 2 + (core + 1) % 2

    def tp_peer(dy, dc):
        return ((y + ny - dy) % ny) * 2 + (core + dc) % 2

    def remote(src, dst, send, recv, **where):
        return pltpu.make_async_remote_copy(
            src_ref=src, dst_ref=dst, send_sem=send, recv_sem=recv,
            device_id=where, device_id_type=MESH,
        )

    barrier = pltpu.get_barrier_semaphore()
    for name, size, me in (("tp", n_tp, tp), ("seg", n_seg, seg), ("dp", n_dp, dp)):
        for o in range(1, size):
            pl.semaphore_signal(
                barrier, inc=1, device_id={name: (me + o) % size}, device_id_type=MESH
            )

    def tok_copy(i):
        part = pl.ds(i * MB, MB)
        return pltpu.make_async_copy(tok_hbm.at[part], tok.at[part], tok_sem.at[i])

    def w_copy(kind, g):
        src = (wq_hbm, wk_hbm, wv_hbm)[kind]
        return pltpu.make_async_copy(
            src.at[:, pl.ds(g * GW, GW)], w.at[kind, g], w_sem.at[kind, g]
        )

    def own_cols(p):
        return pl.ds(pl.multiple_of(p * out_cols, out_cols), out_cols)

    own_copy = pltpu.make_async_copy(wo_hbm.at[:, :, own_cols(tp)], wo.at[0], own_sem)

    tok_copy(0).start()
    w_copy(1, 0).start()
    for i in range(1, rows // MB):
        tok_copy(i).start()
    w_copy(2, 0).start()
    for g in range(1, groups):
        w_copy(1, g).start()
        w_copy(2, g).start()
    for g in range(groups):
        w_copy(0, g).start()
    own_copy.start()

    pl.semaphore_wait(barrier, n_tp - 1 + n_seg - 1 + n_dp - 1)

    mine = dp * sb + pos

    def wo_copy(dy, dc):
        slot = 2 * dy + dc
        peer = tp_peer(dy, dc)
        if dy == 0:
            src, dst = wo_hbm.at[:, :, own_cols(peer)], wo.at[slot]
        else:
            src, dst = wo_hbm.at[mine, :, own_cols(peer)], wo.at[slot, mine]
        return remote(src, dst, wy_send.at[slot], wy_recv.at[slot], tp=peer)

    others = [(dy, dc) for dy in range(1, ny) for dc in range(2)]
    for dy, dc in others:
        wo_copy(dy, dc).start()
    wo_copy(0, 1).start()

    def shard_copy(index, send, **where):
        part = wo.at[pl.ds(2, n_tp - 2), index]
        return remote(part, part, send, shard_recv.at[index], **where)

    def dp_copies(at, step):
        return [
            shard_copy(dp * sb + at, dp_send.at[step, o], dp=(dp + o) % n_dp)
            for o in range(1, n_dp)
        ]

    def shard_step(t, finish=False):
        def go(copy):
            if finish:
                copy.wait_send()
            else:
                copy.start()

        if t == 0:
            if not finish:
                for dy, dc in others:
                    wo_copy(dy, dc).wait_recv()

            @pl.when(pos + 1 < sb)
            def _():
                go(shard_copy(mine, right_send.at[0], seg=seg + 1))

            @pl.when(pos >= 1)
            def _():
                go(shard_copy(mine, left_send.at[0], seg=seg - 1))

            for copy in dp_copies(pos, 0):
                go(copy)
            return

        @pl.when(pos >= t)
        def _():
            index = dp * sb + pos - t
            if not finish:
                shard_copy(index, right_send.at[t], seg=seg).wait_recv()

            @pl.when(pos + 1 < sb)
            def _():
                go(shard_copy(index, right_send.at[t], seg=seg + 1))

            for copy in dp_copies(pos - t, 2 * t - 1):
                go(copy)

        @pl.when(pos + t < sb)
        def _():
            index = dp * sb + pos + t
            if not finish:
                shard_copy(index, left_send.at[t], seg=seg).wait_recv()

            @pl.when(pos >= 1)
            def _():
                go(shard_copy(index, left_send.at[t], seg=seg - 1))

            for copy in dp_copies(pos + t, 2 * t):
                go(copy)

    def mem_copy(g, o):
        return remote(
            mem_out.at[g], mem_in.at[seg, g], mem_send.at[g, o], mem_recv.at[seg, g], seg=seg + o
        )

    def project(kind, g, first=False):
        w_copy(kind, g).wait()

        def body(i, carry):
            if first:
                tok_copy(i).wait()
            part = pl.ds(pl.multiple_of(i * MB, MB), MB)
            val = contract(tok[part, :], w[kind, g], ((1,), (0,))).astype(BF)
            (q, k, v)[kind][g, part, :] = val
            if kind == 1:
                kf[part, :] = features(val.astype(F32)).astype(BF)
            return carry

        lax.fori_loop(0, rows // MB, body, 0)

    def send_delta(g):
        both = contract(kf[...], v[g], ((0,), (0,)))
        mem_out[g, :DH, :] = both[:DH, :DH].astype(BF)
        mem_out[g, DH:GW, :] = both[DH:, DH:].astype(BF)
        norm = jnp.sum(kf[...].astype(F32), axis=0, keepdims=True)
        row = lax.broadcasted_iota(jnp.int32, (16, DH), 0)
        tail = jnp.where(row == 0, norm[:, :DH], jnp.where(row == 1, norm[:, DH:], 0.0))
        tail = jnp.where(row == 2, keep_ref[...], tail)
        mem_out[g, GW:, :] = tail.astype(BF)
        for o in range(1, n_seg):
            @pl.when(seg + o < n_seg)
            def _():
                mem_copy(g, o).start()

    def take_state(g):
        def body(j, state):
            mem, norm = state
            remote(
                mem_out.at[g], mem_in.at[j, g], mem_send.at[g, 0], mem_recv.at[j, g], seg=seg
            ).wait_recv()
            tail = mem_in[j, g, GW:, :].astype(F32)
            held = tail[2:3, :]
            return held * mem + mem_in[j, g, :GW, :].astype(F32), held * norm + tail

        mem, norm = lax.fori_loop(
            0, seg, body, (jnp.zeros((GW, DH), F32), jnp.zeros((16, DH), F32))
        )
        mem = keep_ref[...] * mem
        norm = keep_ref[...] * norm
        row = lax.broadcasted_iota(jnp.int32, (GW, DH), 0)
        read[:, :DH] = jnp.where(row < DH, mem, 0.0).astype(BF)
        read[:, DH:GW] = jnp.where(row < DH, 0.0, mem).astype(BF)
        first = jnp.broadcast_to(norm[0:1, :], (DH, DH)).T.astype(BF)
        second = jnp.broadcast_to(norm[1:2, :], (DH, DH)).T.astype(BF)
        nil = jnp.zeros((DH, DH), BF)
        read[:DH, GW : GW + DH] = first
        read[DH:, GW : GW + DH] = nil
        read[:DH, GW + DH :] = nil
        read[DH:, GW + DH :] = second

    def piece(ref, slot, g, r):
        return ref.at[slot, g, pl.ds(r * RB, RB)]

    def at_copy(dy, g, r):
        slot = 2 * dy if dy else 1
        peer = tp_peer(dy, 0) if dy else sibling
        return remote(
            piece(attn, 0, g, r), piece(attn, slot, g, r),
            at_send.at[dy, g, r], at_recv.at[slot, g, r], tp=peer,
        )

    def fw_copy(dy, g, r):
        return remote(
            piece(attn, 2 * dy, g, r), piece(attn, 2 * dy + 1, g, r),
            fw_send.at[dy, g, r], at_recv.at[2 * dy + 1, g, r], tp=sibling,
        )

    row_at = lax.broadcasted_iota(jnp.int32, (RB, RB), 0)
    col_at = lax.broadcasted_iota(jnp.int32, (RB, RB), 1)

    def attend(g, r):
        part = pl.ds(r * RB, RB)
        query = q[g, part, :]
        qf = features(query.astype(F32)).astype(BF)
        both = contract(qf, read[...], ((1,), (0,)))
        mem_att = both[:, :GW] / jnp.maximum(both[:, GW:], 1.0)
        gate = gate_ref[:, g * GW : (g + 1) * GW]
        local = []
        for h in range(2):
            lanes = slice(h * DH, (h + 1) * DH)
            qh = query[:, lanes]
            near = contract(qh, k[g, part, lanes], ((1,), (1,)))
            near = jnp.where(row_at >= col_at, near, -jnp.inf)
            peak = jnp.max(near, axis=-1, keepdims=True)
            if r:
                far = contract(qh, k[g, : r * RB, lanes], ((1,), (1,)))
                peak = jnp.maximum(peak, jnp.max(far, axis=-1, keepdims=True))
            probs = jnp.exp2((near - peak) * SCALE).astype(BF)
            ones = jnp.ones((RB, DH), BF)
            summed = contract(
                probs, jnp.concatenate([v[g, part, lanes], ones], axis=1), ((1,), (0,))
            )
            if r:
                probs = jnp.exp2((far - peak) * SCALE).astype(BF)
                ones = jnp.ones((r * RB, DH), BF)
                summed += contract(
                    probs, jnp.concatenate([v[g, : r * RB, lanes], ones], axis=1), ((1,), (0,))
                )
            local.append(summed[:, :DH] / summed[:, DH:])
        local = jnp.concatenate(local, axis=1)
        attn[0, g, part, :] = (gate * mem_att + (1.0 - gate) * local).astype(BF)
        for dy in range(ny - 1, -1, -1):
            at_copy(dy, g, r).start()

    project(1, 0, first=True)
    project(2, 0)
    send_delta(0)
    for g in range(1, groups):
        project(1, g)
        if g == 1:
            shard_step(0)
        project(2, g)
        send_delta(g)
    if groups == 1:
        shard_step(0)
    step = 1
    for g in range(groups):
        project(0, g)
        take_state(g)
        for r in range(blocks):
            attend(g, r)
        if step < sb:
            shard_step(step)
            step += 1

    def wo_rows(slot, g):
        per = GW // wo.shape[2]
        return wo[slot, g * per : (g + 1) * per].reshape(GW, out_cols)

    own_copy.wait()
    wo_copy(0, 1).wait_recv()
    for r in range(blocks):
        part = pl.ds(r * RB, RB)
        total = None
        for slot in range(2):
            for g in range(groups):
                if slot:
                    at_copy(0, g, r).wait_recv()
                term = contract(attn[slot, g, part, :], wo_rows(slot, g), ((1,), (0,)))
                total = term if total is None else total + term
        acc[part, :] = total

    while step < sb:
        shard_step(step)
        step += 1
    for o in range(1, n_dp):
        for b in range(sb):
            index = ((dp + o) % n_dp) * sb + b
            shard_copy(index, dp_send.at[0, o], dp=(dp + o) % n_dp).wait_recv()

    def out_copy(r):
        part = pl.ds(r * RB, RB)
        return pltpu.make_async_copy(out.at[part], out_hbm.at[part], out_sem.at[r])

    order = [(g, r) for g in range(groups) for r in range(blocks)]

    def add(slot, g, r):
        part = pl.ds(r * RB, RB)
        acc[part, :] += contract(attn[slot, g, part, :], wo_rows(slot, g), ((1,), (0,)))

    def add_forwarded(g, r):
        for dy in range(1, ny):
            fw_copy(dy, g, r).wait_recv()
            add(2 * dy + 1, g, r)
        if g == groups - 1:
            part = pl.ds(r * RB, RB)
            out[part, :] = acc[part, :].astype(BF)
            out_copy(r).start()

    for n, (g, r) in enumerate(order):
        for dy in range(1, ny):
            at_copy(dy, g, r).wait_recv()
            fw_copy(dy, g, r).start()
            add(2 * dy, g, r)
        if n:
            add_forwarded(*order[n - 1])
    add_forwarded(*order[-1])

    for r in range(blocks):
        out_copy(r).wait()
    for dy, dc in others + [(0, 1)]:
        wo_copy(dy, dc).wait_send()
    for t in range(sb):
        shard_step(t, finish=True)
    for g in range(groups):
        for o in range(1, n_seg):
            @pl.when(seg + o < n_seg)
            def _():
                mem_copy(g, o).wait_send()
    for g, r in order:
        for dy in range(ny):
            at_copy(dy, g, r).wait_send()
        for dy in range(1, ny):
            fw_copy(dy, g, r).wait_send()


def on_device(sizes, tokens, w_query, w_key, w_value, w_out, mem_gate, resets):
    n_seg, n_tp, n_dp = sizes
    rows, width = tokens.shape
    depth = w_out.shape[0]
    groups = depth // GW
    out_cols = w_out.shape[1] // n_tp
    blocks = rows // RB
    sb = n_seg
    while n_seg % sb or depth % (n_dp * sb * 16):
        sb -= 1
    shards = n_dp * sb
    gate = jnp.repeat(jax.nn.sigmoid(mem_gate), DH)[None, :]
    keep = jnp.broadcast_to(1.0 - resets.astype(F32)[:, None], (1, DH))
    dma = pltpu.SemaphoreType.DMA
    hbm = pl.BlockSpec(memory_space=pl.ANY)
    vmem = pl.BlockSpec(memory_space=pltpu.VMEM)
    flops = 2 * rows * width * depth * 4 + 4 * rows * rows * depth
    return pl.pallas_call(
        functools.partial(kernel, n_seg, n_tp, n_dp, sb),
        out_shape=jax.ShapeDtypeStruct((rows, out_cols), BF),
        in_specs=[hbm] * 5 + [vmem] * 2,
        out_specs=hbm,
        scratch_shapes=[
            pltpu.VMEM((rows, width), BF),
            pltpu.VMEM((3, groups, width, GW), BF),
            pltpu.VMEM((n_tp, shards, depth // shards, out_cols), BF),
            pltpu.VMEM((groups, rows, GW), BF),
            pltpu.VMEM((groups, rows, GW), BF),
            pltpu.VMEM((groups, rows, GW), BF),
            pltpu.VMEM((rows, GW), BF),
            pltpu.VMEM((groups, GW + 16, DH), BF),
            pltpu.VMEM((n_seg, groups, GW + 16, DH), BF),
            pltpu.VMEM((GW, 2 * GW), BF),
            pltpu.VMEM((n_tp, groups, rows, GW), BF),
            pltpu.VMEM((rows, out_cols), F32),
            pltpu.VMEM((rows, out_cols), BF),
            dma((rows // MB,)),
            dma((3, groups)),
            dma(()),
            dma((blocks,)),
            dma((n_tp,)),
            dma((n_tp,)),
            dma((sb,)),
            dma((sb,)),
            dma((2 * sb, n_dp)),
            dma((shards,)),
            dma((groups, n_seg)),
            dma((n_seg, groups)),
            dma((n_tp // 2, groups, blocks)),
            dma((n_tp, groups, blocks)),
            dma((n_tp // 2, groups, blocks)),
        ],
        compiler_params=pltpu.CompilerParams(
            collective_id=0, has_side_effects=True, vmem_limit_bytes=60 * 1024 * 1024
        ),
        cost_estimate=pl.CostEstimate(
            flops=flops, bytes_accessed=4 * width * depth * 2 + rows * width * 2, transcendentals=0
        ),
    )(tokens, w_query, w_key, w_value, w_out.reshape(shards, depth // shards, width), gate, keep)


def solution(mesh):
    placed = (
        P(("dp", "seg"), None),
        P(None, "tp"),
        P(None, "tp"),
        P(None, "tp"),
        P("tp", None),
        P("tp"),
        P(("dp", "seg")),
    )
    sizes = (mesh.shape["seg"], mesh.shape["tp"], mesh.shape["dp"])
    return jax.shard_map(
        functools.partial(on_device, sizes),
        mesh=mesh, in_specs=placed, out_specs=P(("dp", "seg"), "tp"), check_vma=False,
    )
```

```python
import functools
import math

import jax
import jax.numpy as jnp
from jax import lax
from jax.experimental import pallas as pl
from jax.experimental.pallas import tpu as pltpu
from jax.sharding import PartitionSpec as P

DH = 128
GW = 2 * DH
RB = 256
MB = 512
MESH = pl.DeviceIdType.MESH
F32 = jnp.float32
BF = jnp.bfloat16
SCALE = math.log2(math.e) / math.sqrt(DH)


def features(field):
    return jnp.where(field > 0, field + 1.0, jnp.exp(jnp.minimum(field, 0.0)))


def contract(a, b, dims):
    return lax.dot_general(a, b, (dims, ((), ())), preferred_element_type=F32)


def kernel(
    n_seg, n_tp, n_dp, sb,
    tok_hbm, wq_hbm, wk_hbm, wv_hbm, wo_hbm, gate_ref, reset_ref,
    out_hbm,
    tok, w, wo, q, k, v, kf, mem_out, mem_in, read, attn, acc, out,
    tok_sem, w_sem, own_sem, out_sem,
    wy_send, wy_recv, right_send, left_send, dp_send, shard_recv,
    mem_send, mem_recv, at_send, at_recv, fw_send,
):
    seg = lax.axis_index("seg")
    tp = lax.axis_index("tp")
    dp = lax.axis_index("dp")
    ny = n_tp // 2
    y, core = tp // 2, tp % 2
    rows = tok.shape[0]
    groups = q.shape[0]
    blocks = rows // RB
    out_cols = out.shape[1]
    pos = seg % sb
    sibling = y * 2 + (core + 1) % 2

    def tp_peer(dy, dc):
        return ((y + ny - dy) % ny) * 2 + (core + dc) % 2

    def remote(src, dst, send, recv, **where):
        return pltpu.make_async_remote_copy(
            src_ref=src, dst_ref=dst, send_sem=send, recv_sem=recv,
            device_id=where, device_id_type=MESH,
        )

    barrier = pltpu.get_barrier_semaphore()
    for name, size, me in (("tp", n_tp, tp), ("seg", n_seg, seg), ("dp", n_dp, dp)):
        for o in range(1, size):
            pl.semaphore_signal(
                barrier, inc=1, device_id={name: (me + o) % size}, device_id_type=MESH
            )

    def tok_copy(i):
        part = pl.ds(i * MB, MB)
        return pltpu.make_async_copy(tok_hbm.at[part], tok.at[part], tok_sem.at[i])

    def column(kind, g):
        return (3 * g + (2, 0, 1)[kind]) * GW

    def w_copy(kind, g):
        src = (wq_hbm, wk_hbm, wv_hbm)[kind]
        return pltpu.make_async_copy(
            src.at[:, pl.ds(g * GW, GW)], w.at[:, pl.ds(column(kind, g), GW)], w_sem.at[kind, g]
        )

    def own_cols(p):
        return pl.ds(pl.multiple_of(p * out_cols, out_cols), out_cols)

    own_copy = pltpu.make_async_copy(wo_hbm.at[:, :, own_cols(tp)], wo.at[0], own_sem)

    tok_copy(0).start()
    w_copy(1, 0).start()
    for i in range(1, rows // MB):
        tok_copy(i).start()
    w_copy(2, 0).start()
    w_copy(0, 0).start()
    for g in range(1, groups):
        for kind in (1, 2, 0):
            w_copy(kind, g).start()
    own_copy.start()

    pl.semaphore_wait(barrier, n_tp - 1 + n_seg - 1 + n_dp - 1)

    mine = dp * sb + pos

    def wo_copy(dy, dc):
        slot = 2 * dy + dc
        peer = tp_peer(dy, dc)
        if dy == 0:
            src, dst = wo_hbm.at[:, :, own_cols(peer)], wo.at[slot]
        else:
            src, dst = wo_hbm.at[mine, :, own_cols(peer)], wo.at[slot, mine]
        return remote(src, dst, wy_send.at[slot], wy_recv.at[slot], tp=peer)

    others = [(dy, dc) for dy in range(1, ny) for dc in range(2)]
    for dy, dc in others:
        wo_copy(dy, dc).start()
    wo_copy(0, 1).start()

    def shard_copy(index, send, **where):
        part = wo.at[pl.ds(2, n_tp - 2), index]
        return remote(part, part, send, shard_recv.at[index], **where)

    def dp_copies(at, step):
        return [
            shard_copy(dp * sb + at, dp_send.at[step, o], dp=(dp + o) % n_dp)
            for o in range(1, n_dp)
        ]

    def shard_step(t, finish=False):
        def go(copy):
            if finish:
                copy.wait_send()
            else:
                copy.start()

        if t == 0:
            if not finish:
                for dy, dc in others:
                    wo_copy(dy, dc).wait_recv()

            @pl.when(pos + 1 < sb)
            def _():
                go(shard_copy(mine, right_send.at[0], seg=seg + 1))

            @pl.when(pos >= 1)
            def _():
                go(shard_copy(mine, left_send.at[0], seg=seg - 1))

            for copy in dp_copies(pos, 0):
                go(copy)
            return

        @pl.when(pos >= t)
        def _():
            index = dp * sb + pos - t
            if not finish:
                shard_copy(index, right_send.at[t], seg=seg).wait_recv()

            @pl.when(pos + 1 < sb)
            def _():
                go(shard_copy(index, right_send.at[t], seg=seg + 1))

            for copy in dp_copies(pos - t, 2 * t - 1):
                go(copy)

        @pl.when(pos + t < sb)
        def _():
            index = dp * sb + pos + t
            if not finish:
                shard_copy(index, left_send.at[t], seg=seg).wait_recv()

            @pl.when(pos >= 1)
            def _():
                go(shard_copy(index, left_send.at[t], seg=seg - 1))

            for copy in dp_copies(pos + t, 2 * t):
                go(copy)

    def mem_copy(g, o):
        return remote(
            mem_out.at[g], mem_in.at[seg, g], mem_send.at[g, o], mem_recv.at[seg, g], seg=seg + o
        )

    def project(parts, first=False, midway=None):
        for kind, g in parts:
            w_copy(kind, g).wait()
        start = column(*parts[0])
        stop = start + len(parts) * GW
        for i in range(rows // MB):
            if first:
                tok_copy(i).wait()
            if midway is not None and i == 1:
                midway()
            part = pl.ds(i * MB, MB)
            wide = contract(tok[part, :], w[:, start:stop], ((1,), (0,))).astype(BF)
            for n, (kind, g) in enumerate(parts):
                val = wide[:, n * GW : (n + 1) * GW]
                (q, k, v)[kind][g, part, :] = val
                if kind == 1:
                    kf[part, :] = features(val.astype(F32)).astype(BF)

    keep = jnp.full((1, DH), 1.0 - reset_ref[0].astype(F32), F32)

    def send_delta(g):
        both = contract(kf[...], v[g], ((0,), (0,)))
        mem_out[g, :DH, :] = both[:DH, :DH].astype(BF)
        mem_out[g, DH:GW, :] = both[DH:, DH:].astype(BF)
        norm = jnp.sum(kf[...].astype(F32), axis=0, keepdims=True)
        row = lax.broadcasted_iota(jnp.int32, (16, DH), 0)
        tail = jnp.where(row == 0, norm[:, :DH], jnp.where(row == 1, norm[:, DH:], 0.0))
        tail = jnp.where(row == 2, keep, tail)
        mem_out[g, GW:, :] = tail.astype(BF)
        for o in range(1, n_seg):
            @pl.when(seg + o < n_seg)
            def _():
                mem_copy(g, o).start()

    def take_state(g):
        def body(j, state):
            mem, norm = state
            remote(
                mem_out.at[g], mem_in.at[j, g], mem_send.at[g, 0], mem_recv.at[j, g], seg=seg
            ).wait_recv()
            tail = mem_in[j, g, GW:, :].astype(F32)
            held = tail[2:3, :]
            return held * mem + mem_in[j, g, :GW, :].astype(F32), held * norm + tail

        mem, norm = lax.fori_loop(
            0, seg, body, (jnp.zeros((GW, DH), F32), jnp.zeros((16, DH), F32))
        )
        mem = keep * mem
        norm = keep * norm
        row = lax.broadcasted_iota(jnp.int32, (GW, DH), 0)
        read[:, :DH] = jnp.where(row < DH, mem, 0.0).astype(BF)
        read[:, DH:GW] = jnp.where(row < DH, 0.0, mem).astype(BF)
        first = jnp.broadcast_to(norm[0:1, :], (DH, DH)).T.astype(BF)
        second = jnp.broadcast_to(norm[1:2, :], (DH, DH)).T.astype(BF)
        nil = jnp.zeros((DH, DH), BF)
        read[:DH, GW : GW + DH] = first
        read[DH:, GW : GW + DH] = nil
        read[:DH, GW + DH :] = nil
        read[DH:, GW + DH :] = second

    def piece(ref, slot, g, r):
        return ref.at[slot, g, pl.ds(r * RB, RB)]

    def at_copy(dy, g, r):
        slot = 2 * dy if dy else 1
        peer = tp_peer(dy, 0) if dy else sibling
        return remote(
            piece(attn, 0, g, r), piece(attn, slot, g, r),
            at_send.at[dy, g, r], at_recv.at[slot, g, r], tp=peer,
        )

    def fw_copy(dy, g, r):
        return remote(
            piece(attn, 2 * dy, g, r), piece(attn, 2 * dy + 1, g, r),
            fw_send.at[dy, g, r], at_recv.at[2 * dy + 1, g, r], tp=sibling,
        )

    gate_row = jax.nn.sigmoid(
        jnp.concatenate([jnp.full((1, DH), gate_ref[n], F32) for n in range(2 * groups)], axis=1)
    )
    row_at = lax.broadcasted_iota(jnp.int32, (RB, RB), 0)
    col_at = lax.broadcasted_iota(jnp.int32, (RB, RB), 1)

    def attend(g, r):
        part = pl.ds(r * RB, RB)
        query = q[g, part, :]
        qf = features(query.astype(F32)).astype(BF)
        both = contract(qf, read[...], ((1,), (0,)))
        mem_att = both[:, :GW] / jnp.maximum(both[:, GW:], 1.0)
        gate = gate_row[:, g * GW : (g + 1) * GW]
        local = []
        for h in range(2):
            lanes = slice(h * DH, (h + 1) * DH)
            qh = query[:, lanes]
            near = contract(qh, k[g, part, lanes], ((1,), (1,)))
            near = jnp.where(row_at >= col_at, near, -jnp.inf)
            peak = jnp.max(near, axis=-1, keepdims=True)
            if r:
                far = contract(qh, k[g, : r * RB, lanes], ((1,), (1,)))
                peak = jnp.maximum(peak, jnp.max(far, axis=-1, keepdims=True))
            probs = jnp.exp2((near - peak) * SCALE).astype(BF)
            ones = jnp.ones((RB, DH), BF)
            summed = contract(
                probs, jnp.concatenate([v[g, part, lanes], ones], axis=1), ((1,), (0,))
            )
            if r:
                probs = jnp.exp2((far - peak) * SCALE).astype(BF)
                ones = jnp.ones((r * RB, DH), BF)
                summed += contract(
                    probs, jnp.concatenate([v[g, : r * RB, lanes], ones], axis=1), ((1,), (0,))
                )
            local.append(summed[:, :DH] / summed[:, DH:])
        local = jnp.concatenate(local, axis=1)
        attn[0, g, part, :] = (gate * mem_att + (1.0 - gate) * local).astype(BF)
        for dy in range(ny - 1, -1, -1):
            at_copy(dy, g, r).start()

    def wo_rows(slot, g):
        per = GW // wo.shape[2]
        return wo[slot, g * per : (g + 1) * per].reshape(GW, out_cols)

    def near_out(g):
        for r in range(blocks):
            part = pl.ds(r * RB, RB)
            at_copy(0, g, r).wait_recv()
            total = contract(attn[0, g, part, :], wo_rows(0, g), ((1,), (0,)))
            total += contract(attn[1, g, part, :], wo_rows(1, g), ((1,), (0,)))
            if g:
                total += acc[part, :]
            acc[part, :] = total

    pending = list(range(sb))

    def hop():
        if pending:
            shard_step(pending.pop(0))

    for g in range(groups):
        if g == 0:
            project([(1, 0), (2, 0)], first=True)
            send_delta(0)
            nexts = [(0, 0)] + ([(1, 1)] if groups > 1 else [])
            project(nexts, midway=hop)
        else:
            project([(2, g)])
            send_delta(g)
            project([(0, g)] + ([(1, g + 1)] if g + 1 < groups else []))
            if g == 1:
                own_copy.wait()
                wo_copy(0, 1).wait_recv()
            near_out(g - 1)
            hop()
        take_state(g)
        for r in range(blocks):
            attend(g, r)
        hop()
    if groups == 1:
        own_copy.wait()
        wo_copy(0, 1).wait_recv()
    near_out(groups - 1)
    while pending:
        hop()
    for o in range(1, n_dp):
        for b in range(sb):
            index = ((dp + o) % n_dp) * sb + b
            shard_copy(index, dp_send.at[0, o], dp=(dp + o) % n_dp).wait_recv()

    def out_copy(r):
        part = pl.ds(r * RB, RB)
        return pltpu.make_async_copy(out.at[part], out_hbm.at[part], out_sem.at[r])

    order = [(g, r) for g in range(groups) for r in range(blocks)]

    def add(slot, g, r):
        part = pl.ds(r * RB, RB)
        acc[part, :] += contract(attn[slot, g, part, :], wo_rows(slot, g), ((1,), (0,)))

    def add_forwarded(g, r):
        for dy in range(1, ny):
            fw_copy(dy, g, r).wait_recv()
            add(2 * dy + 1, g, r)
        if g == groups - 1:
            part = pl.ds(r * RB, RB)
            out[part, :] = acc[part, :].astype(BF)
            out_copy(r).start()

    for n, (g, r) in enumerate(order):
        for dy in range(1, ny):
            at_copy(dy, g, r).wait_recv()
            fw_copy(dy, g, r).start()
            add(2 * dy, g, r)
        if n:
            add_forwarded(*order[n - 1])
    add_forwarded(*order[-1])

    for r in range(blocks):
        out_copy(r).wait()
    for dy, dc in others + [(0, 1)]:
        wo_copy(dy, dc).wait_send()
    for t in range(sb):
        shard_step(t, finish=True)
    for g in range(groups):
        for o in range(1, n_seg):
            @pl.when(seg + o < n_seg)
            def _():
                mem_copy(g, o).wait_send()
    for g, r in order:
        for dy in range(ny):
            at_copy(dy, g, r).wait_send()
        for dy in range(1, ny):
            fw_copy(dy, g, r).wait_send()


def on_device(sizes, tokens, w_query, w_key, w_value, w_out, mem_gate, resets):
    n_seg, n_tp, n_dp = sizes
    rows, width = tokens.shape
    depth = w_out.shape[0]
    groups = depth // GW
    out_cols = w_out.shape[1] // n_tp
    blocks = rows // RB
    sb = n_seg
    while n_seg % sb or depth % (n_dp * sb * 16):
        sb -= 1
    shards = n_dp * sb
    dma = pltpu.SemaphoreType.DMA
    hbm = pl.BlockSpec(memory_space=pl.ANY)
    smem = pl.BlockSpec(memory_space=pltpu.SMEM)
    flops = 2 * rows * width * depth * 4 + 4 * rows * rows * depth
    return pl.pallas_call(
        functools.partial(kernel, n_seg, n_tp, n_dp, sb),
        out_shape=jax.ShapeDtypeStruct((rows, out_cols), BF),
        in_specs=[hbm] * 5 + [smem] * 2,
        out_specs=hbm,
        scratch_shapes=[
            pltpu.VMEM((rows, width), BF),
            pltpu.VMEM((width, 3 * groups * GW), BF),
            pltpu.VMEM((n_tp, shards, depth // shards, out_cols), BF),
            pltpu.VMEM((groups, rows, GW), BF),
            pltpu.VMEM((groups, rows, GW), BF),
            pltpu.VMEM((groups, rows, GW), BF),
            pltpu.VMEM((rows, GW), BF),
            pltpu.VMEM((groups, GW + 16, DH), BF),
            pltpu.VMEM((n_seg, groups, GW + 16, DH), BF),
            pltpu.VMEM((GW, 2 * GW), BF),
            pltpu.VMEM((n_tp, groups, rows, GW), BF),
            pltpu.VMEM((rows, out_cols), F32),
            pltpu.VMEM((rows, out_cols), BF),
            dma((rows // MB,)),
            dma((3, groups)),
            dma(()),
            dma((blocks,)),
            dma((n_tp,)),
            dma((n_tp,)),
            dma((sb,)),
            dma((sb,)),
            dma((2 * sb, n_dp)),
            dma((shards,)),
            dma((groups, n_seg)),
            dma((n_seg, groups)),
            dma((n_tp // 2, groups, blocks)),
            dma((n_tp, groups, blocks)),
            dma((n_tp // 2, groups, blocks)),
        ],
        compiler_params=pltpu.CompilerParams(
            collective_id=0, has_side_effects=True, vmem_limit_bytes=60 * 1024 * 1024
        ),
        cost_estimate=pl.CostEstimate(
            flops=flops, bytes_accessed=4 * width * depth * 2 + rows * width * 2, transcendentals=0
        ),
    )(tokens, w_query, w_key, w_value, w_out.reshape(shards, depth // shards, width), mem_gate, resets)


def solution(mesh):
    placed = (
        P(("dp", "seg"), None),
        P(None, "tp"),
        P(None, "tp"),
        P(None, "tp"),
        P("tp", None),
        P("tp"),
        P(("dp", "seg")),
    )
    sizes = (mesh.shape["seg"], mesh.shape["tp"], mesh.shape["dp"])
    return jax.shard_map(
        functools.partial(on_device, sizes),
        mesh=mesh, in_specs=placed, out_specs=P(("dp", "seg"), "tp"), check_vma=False,
    )
```

```python
import functools
import math

import jax
import jax.numpy as jnp
from jax import lax
from jax.experimental import pallas as pl
from jax.experimental.pallas import tpu as pltpu
from jax.sharding import PartitionSpec as P

DH = 128
GW = 2 * DH
RB = 256
MB = 512
MESH = pl.DeviceIdType.MESH
F32 = jnp.float32
BF = jnp.bfloat16
SCALE = math.log2(math.e) / math.sqrt(DH)


def features(field):
    return jnp.where(field > 0, field + 1.0, jnp.exp(jnp.minimum(field, 0.0)))


def contract(a, b, dims):
    return lax.dot_general(a, b, (dims, ((), ())), preferred_element_type=F32)


def kernel(
    n_seg, n_tp, n_dp, sb,
    tok_hbm, wq_hbm, wk_hbm, wv_hbm, wo_hbm, gate_ref, reset_ref,
    out_hbm,
    tok, w, wo, q, k, v, kf, mem_out, mem_in, read, attn, acc, out,
    tok_sem, w_sem, own_sem, out_sem,
    wy_send, wy_recv, pair_send, dp_send, shard_recv,
    mem_send, mem_recv, at_send, at_recv, fw_send,
):
    seg = lax.axis_index("seg")
    tp = lax.axis_index("tp")
    dp = lax.axis_index("dp")
    ny = n_tp // 2
    y, core = tp // 2, tp % 2
    rows = tok.shape[0]
    groups = q.shape[0]
    blocks = rows // RB
    out_cols = out.shape[1]
    pos = seg % sb
    sibling = y * 2 + (core + 1) % 2

    def tp_peer(dy, dc):
        return ((y + ny - dy) % ny) * 2 + (core + dc) % 2

    def remote(src, dst, send, recv, **where):
        return pltpu.make_async_remote_copy(
            src_ref=src, dst_ref=dst, send_sem=send, recv_sem=recv,
            device_id=where, device_id_type=MESH,
        )

    barrier = pltpu.get_barrier_semaphore()
    for name, size, me in (("tp", n_tp, tp), ("seg", n_seg, seg), ("dp", n_dp, dp)):
        for o in range(1, size):
            pl.semaphore_signal(
                barrier, inc=1, device_id={name: (me + o) % size}, device_id_type=MESH
            )

    def tok_copy(i):
        part = pl.ds(i * MB, MB)
        return pltpu.make_async_copy(tok_hbm.at[part], tok.at[part], tok_sem.at[i])

    def column(kind, g):
        return (3 * g + (2, 0, 1)[kind]) * GW

    def w_copy(kind, g):
        src = (wq_hbm, wk_hbm, wv_hbm)[kind]
        return pltpu.make_async_copy(
            src.at[:, pl.ds(g * GW, GW)], w.at[:, pl.ds(column(kind, g), GW)], w_sem.at[kind, g]
        )

    def own_cols(p):
        return pl.ds(pl.multiple_of(p * out_cols, out_cols), out_cols)

    own_copy = pltpu.make_async_copy(wo_hbm.at[:, :, own_cols(tp)], wo.at[0], own_sem)

    tok_copy(0).start()
    w_copy(1, 0).start()
    for i in range(1, rows // MB):
        tok_copy(i).start()
    w_copy(2, 0).start()
    w_copy(0, 0).start()
    for g in range(1, groups):
        for kind in (1, 2, 0):
            w_copy(kind, g).start()
    own_copy.start()

    pl.semaphore_wait(barrier, n_tp - 1 + n_seg - 1 + n_dp - 1)

    mine = dp * sb + pos

    def wo_copy(dy, dc):
        slot = 2 * dy + dc
        peer = tp_peer(dy, dc)
        if dy == 0:
            src, dst = wo_hbm.at[:, :, own_cols(peer)], wo.at[slot]
        else:
            src, dst = wo_hbm.at[mine, :, own_cols(peer)], wo.at[slot, mine]
        return remote(src, dst, wy_send.at[slot], wy_recv.at[slot], tp=peer)

    others = [(dy, dc) for dy in range(1, ny) for dc in range(2)]
    for dy, dc in others:
        wo_copy(dy, dc).start()
    wo_copy(0, 1).start()

    pair = dp * sb + (pos + 1) % sb
    partner = seg + 1 - 2 * pos
    half = (n_tp - 2) // 2

    def shard_copy(part, index, send, **where):
        block = wo.at[pl.ds(2 + part * half, half), index]
        return remote(block, block, send, shard_recv.at[part, index], **where)

    def to_pair(part, index, step):
        return shard_copy(part, index, pair_send.at[part, step], seg=partner)

    def to_dp(part, index, step):
        return [
            shard_copy(part, index, dp_send.at[part, step, o], dp=(dp + o) % n_dp)
            for o in range(1, n_dp)
        ]

    def across(o):
        return ((dp + o) % n_dp) * sb + pos

    def own_shard(part):
        for dy, dc in others[part * half : (part + 1) * half]:
            wo_copy(dy, dc).wait_recv()
        to_pair(part, mine, 0).start()
        for copy in to_dp(part, mine, 0):
            copy.start()

    def pass_on(part):
        if part == 0:
            to_pair(0, pair, 0).wait_recv()
            for copy in to_dp(0, pair, 1):
                copy.start()
        else:
            for o in range(1, n_dp):
                to_pair(1, across(o), 0).wait_recv()
                to_pair(1, across(o), o).start()

    def all_shards():
        to_pair(1, pair, 0).wait_recv()
        for o in range(1, n_dp):
            other = ((dp + o) % n_dp) * sb + (pos + 1) % sb
            to_pair(0, across(o), 0).wait_recv()
            to_pair(0, other, 0).wait_recv()
            to_pair(1, other, 0).wait_recv()

    def shards_sent():
        for part in range(2):
            to_pair(part, mine, 0).wait_send()
            for copy in to_dp(part, mine, 0):
                copy.wait_send()
        for copy in to_dp(0, pair, 1):
            copy.wait_send()
        for o in range(1, n_dp):
            to_pair(1, across(o), o).wait_send()

    def mem_copy(g, o):
        return remote(
            mem_out.at[g], mem_in.at[seg, g], mem_send.at[g, o], mem_recv.at[seg, g], seg=seg + o
        )

    def project(parts, first=False, midway=None):
        for kind, g in parts:
            w_copy(kind, g).wait()
        start = column(*parts[0])
        stop = start + len(parts) * GW
        for i in range(rows // MB):
            if first:
                tok_copy(i).wait()
            if midway is not None and i == 1:
                midway()
            part = pl.ds(i * MB, MB)
            wide = contract(tok[part, :], w[:, start:stop], ((1,), (0,))).astype(BF)
            for n, (kind, g) in enumerate(parts):
                val = wide[:, n * GW : (n + 1) * GW]
                (q, k, v)[kind][g, part, :] = val
                if kind == 1:
                    kf[part, :] = features(val.astype(F32)).astype(BF)

    keep = jnp.full((1, DH), 1.0 - reset_ref[0].astype(F32), F32)

    def send_delta(g):
        both = contract(kf[...], v[g], ((0,), (0,)))
        mem_out[g, :DH, :] = both[:DH, :DH].astype(BF)
        mem_out[g, DH:GW, :] = both[DH:, DH:].astype(BF)
        norm = jnp.sum(kf[...].astype(F32), axis=0, keepdims=True)
        row = lax.broadcasted_iota(jnp.int32, (16, DH), 0)
        tail = jnp.where(row == 0, norm[:, :DH], jnp.where(row == 1, norm[:, DH:], 0.0))
        tail = jnp.where(row == 2, keep, tail)
        mem_out[g, GW:, :] = tail.astype(BF)
        for o in range(1, n_seg):
            @pl.when(seg + o < n_seg)
            def _():
                mem_copy(g, o).start()

    def take_state(g):
        def body(j, state):
            mem, norm = state
            remote(
                mem_out.at[g], mem_in.at[j, g], mem_send.at[g, 0], mem_recv.at[j, g], seg=seg
            ).wait_recv()
            tail = mem_in[j, g, GW:, :].astype(F32)
            held = tail[2:3, :]
            return held * mem + mem_in[j, g, :GW, :].astype(F32), held * norm + tail

        mem, norm = lax.fori_loop(
            0, seg, body, (jnp.zeros((GW, DH), F32), jnp.zeros((16, DH), F32))
        )
        mem = keep * mem
        norm = keep * norm
        row = lax.broadcasted_iota(jnp.int32, (GW, DH), 0)
        read[:, :DH] = jnp.where(row < DH, mem, 0.0).astype(BF)
        read[:, DH:GW] = jnp.where(row < DH, 0.0, mem).astype(BF)
        first = jnp.broadcast_to(norm[0:1, :], (DH, DH)).T.astype(BF)
        second = jnp.broadcast_to(norm[1:2, :], (DH, DH)).T.astype(BF)
        nil = jnp.zeros((DH, DH), BF)
        read[:DH, GW : GW + DH] = first
        read[DH:, GW : GW + DH] = nil
        read[:DH, GW + DH :] = nil
        read[DH:, GW + DH :] = second

    def piece(ref, slot, g, r):
        return ref.at[slot, g, pl.ds(r * RB, RB)]

    def at_copy(dy, g, r):
        slot = 2 * dy if dy else 1
        peer = tp_peer(dy, 0) if dy else sibling
        return remote(
            piece(attn, 0, g, r), piece(attn, slot, g, r),
            at_send.at[dy, g, r], at_recv.at[slot, g, r], tp=peer,
        )

    def fw_copy(dy, g, r):
        return remote(
            piece(attn, 2 * dy, g, r), piece(attn, 2 * dy + 1, g, r),
            fw_send.at[dy, g, r], at_recv.at[2 * dy + 1, g, r], tp=sibling,
        )

    gate_row = jax.nn.sigmoid(
        jnp.concatenate([jnp.full((1, DH), gate_ref[n], F32) for n in range(2 * groups)], axis=1)
    )
    row_at = lax.broadcasted_iota(jnp.int32, (RB, RB), 0)
    col_at = lax.broadcasted_iota(jnp.int32, (RB, RB), 1)

    def attend(g, r):
        part = pl.ds(r * RB, RB)
        query = q[g, part, :]
        qf = features(query.astype(F32)).astype(BF)
        both = contract(qf, read[...], ((1,), (0,)))
        mem_att = both[:, :GW] / jnp.maximum(both[:, GW:], 1.0)
        gate = gate_row[:, g * GW : (g + 1) * GW]
        local = []
        for h in range(2):
            lanes = slice(h * DH, (h + 1) * DH)
            qh = query[:, lanes]
            near = contract(qh, k[g, part, lanes], ((1,), (1,)))
            near = jnp.where(row_at >= col_at, near, -jnp.inf)
            peak = jnp.max(near, axis=-1, keepdims=True)
            if r:
                far = contract(qh, k[g, : r * RB, lanes], ((1,), (1,)))
                peak = jnp.maximum(peak, jnp.max(far, axis=-1, keepdims=True))
            probs = jnp.exp2((near - peak) * SCALE).astype(BF)
            ones = jnp.ones((RB, DH), BF)
            summed = contract(
                probs, jnp.concatenate([v[g, part, lanes], ones], axis=1), ((1,), (0,))
            )
            if r:
                probs = jnp.exp2((far - peak) * SCALE).astype(BF)
                ones = jnp.ones((r * RB, DH), BF)
                summed += contract(
                    probs, jnp.concatenate([v[g, : r * RB, lanes], ones], axis=1), ((1,), (0,))
                )
            local.append(summed[:, :DH] / summed[:, DH:])
        local = jnp.concatenate(local, axis=1)
        attn[0, g, part, :] = (gate * mem_att + (1.0 - gate) * local).astype(BF)
        for dy in range(ny - 1, -1, -1):
            at_copy(dy, g, r).start()

    def wo_rows(slot, g):
        per = GW // wo.shape[2]
        return wo[slot, g * per : (g + 1) * per].reshape(GW, out_cols)

    def near_out(g):
        for r in range(blocks):
            part = pl.ds(r * RB, RB)
            at_copy(0, g, r).wait_recv()
            total = contract(attn[0, g, part, :], wo_rows(0, g), ((1,), (0,)))
            total += contract(attn[1, g, part, :], wo_rows(1, g), ((1,), (0,)))
            if g:
                total += acc[part, :]
            acc[part, :] = total

    project([(1, 0), (2, 0)], first=True)
    send_delta(0)
    project([(0, 0)] + [(1, 1)] * (groups > 1), midway=lambda: own_shard(0))
    own_shard(1)
    for g in range(groups):
        if g:
            project([(2, g)])
            send_delta(g)
            if g == 1:
                pass_on(0)
            project([(0, g)] + [(1, g + 1)] * (g + 1 < groups))
            if g == 1:
                own_copy.wait()
                wo_copy(0, 1).wait_recv()
                pass_on(1)
            near_out(g - 1)
        take_state(g)
        for r in range(blocks):
            attend(g, r)
    if groups == 1:
        own_copy.wait()
        wo_copy(0, 1).wait_recv()
        pass_on(0)
        pass_on(1)
    near_out(groups - 1)
    all_shards()

    def out_copy(r):
        part = pl.ds(r * RB, RB)
        return pltpu.make_async_copy(out.at[part], out_hbm.at[part], out_sem.at[r])

    order = [(g, r) for g in range(groups) for r in range(blocks)]

    def add(slot, g, r):
        part = pl.ds(r * RB, RB)
        acc[part, :] += contract(attn[slot, g, part, :], wo_rows(slot, g), ((1,), (0,)))

    def add_forwarded(g, r):
        for dy in range(1, ny):
            fw_copy(dy, g, r).wait_recv()
            add(2 * dy + 1, g, r)
        if g == groups - 1:
            part = pl.ds(r * RB, RB)
            out[part, :] = acc[part, :].astype(BF)
            out_copy(r).start()

    for n, (g, r) in enumerate(order):
        for dy in range(1, ny):
            at_copy(dy, g, r).wait_recv()
            fw_copy(dy, g, r).start()
            add(2 * dy, g, r)
        if n:
            add_forwarded(*order[n - 1])
    add_forwarded(*order[-1])

    for r in range(blocks):
        out_copy(r).wait()
    for dy, dc in others + [(0, 1)]:
        wo_copy(dy, dc).wait_send()
    shards_sent()
    for g in range(groups):
        for o in range(1, n_seg):
            @pl.when(seg + o < n_seg)
            def _():
                mem_copy(g, o).wait_send()
    for g, r in order:
        for dy in range(ny):
            at_copy(dy, g, r).wait_send()
        for dy in range(1, ny):
            fw_copy(dy, g, r).wait_send()


def hand_over(src, dst):
    dst[...] = src[...]


def on_device(sizes, tokens, w_query, w_key, w_value, w_out, mem_gate, resets):
    n_seg, n_tp, n_dp = sizes
    rows, width = tokens.shape
    depth = w_out.shape[0]
    groups = depth // GW
    out_cols = w_out.shape[1] // n_tp
    blocks = rows // RB
    sb = 2
    shards = n_dp * sb
    dma = pltpu.SemaphoreType.DMA
    hbm = pl.BlockSpec(memory_space=pl.ANY)
    smem = pl.BlockSpec(memory_space=pltpu.SMEM)
    flops = 2 * rows * width * depth * 4 + 4 * rows * rows * depth
    whole = pl.pallas_call(
        functools.partial(kernel, n_seg, n_tp, n_dp, sb),
        out_shape=jax.ShapeDtypeStruct((rows, out_cols), BF),
        in_specs=[hbm] * 5 + [smem] * 2,
        out_specs=hbm,
        scratch_shapes=[
            pltpu.VMEM((rows, width), BF),
            pltpu.VMEM((width, 3 * groups * GW), BF),
            pltpu.VMEM((n_tp, shards, depth // shards, out_cols), BF),
            pltpu.VMEM((groups, rows, GW), BF),
            pltpu.VMEM((groups, rows, GW), BF),
            pltpu.VMEM((groups, rows, GW), BF),
            pltpu.VMEM((rows, GW), BF),
            pltpu.VMEM((groups, GW + 16, DH), BF),
            pltpu.VMEM((n_seg, groups, GW + 16, DH), BF),
            pltpu.VMEM((GW, 2 * GW), BF),
            pltpu.VMEM((n_tp, groups, rows, GW), BF),
            pltpu.VMEM((rows, out_cols), F32),
            pltpu.VMEM((rows, out_cols), BF),
            dma((rows // MB,)),
            dma((3, groups)),
            dma(()),
            dma((blocks,)),
            dma((n_tp,)),
            dma((n_tp,)),
            dma((2, n_dp)),
            dma((2, 2, n_dp)),
            dma((2, shards)),
            dma((groups, n_seg)),
            dma((n_seg, groups)),
            dma((n_tp // 2, groups, blocks)),
            dma((n_tp, groups, blocks)),
            dma((n_tp // 2, groups, blocks)),
        ],
        compiler_params=pltpu.CompilerParams(
            collective_id=0, has_side_effects=True, vmem_limit_bytes=60 * 1024 * 1024
        ),
        cost_estimate=pl.CostEstimate(
            flops=flops, bytes_accessed=4 * width * depth * 2 + rows * width * 2, transcendentals=0
        ),
    )(tokens, w_query, w_key, w_value, w_out.reshape(shards, depth // shards, width), mem_gate, resets)
    block = pl.BlockSpec((RB, out_cols), lambda i: (i, 0))
    return pl.pallas_call(
        hand_over,
        out_shape=jax.ShapeDtypeStruct((rows, out_cols), BF),
        grid=(blocks,),
        in_specs=[block],
        out_specs=block,
    )(whole)


def solution(mesh):
    placed = (
        P(("dp", "seg"), None),
        P(None, "tp"),
        P(None, "tp"),
        P(None, "tp"),
        P("tp", None),
        P("tp"),
        P(("dp", "seg")),
    )
    sizes = (mesh.shape["seg"], mesh.shape["tp"], mesh.shape["dp"])
    return jax.shard_map(
        functools.partial(on_device, sizes),
        mesh=mesh, in_specs=placed, out_specs=P(("dp", "seg"), "tp"), check_vma=False,
    )
```

```python
import functools
import math

import jax
import jax.numpy as jnp
from jax import lax
from jax.experimental import pallas as pl
from jax.experimental.pallas import tpu as pltpu
from jax.sharding import PartitionSpec as P

DH = 128
GW = 2 * DH
RB = 256
MB = 512
MESH = pl.DeviceIdType.MESH
F32 = jnp.float32
BF = jnp.bfloat16
SCALE = math.log2(math.e) / math.sqrt(DH)


def features(field):
    return jnp.where(field > 0, field + 1.0, jnp.exp(jnp.minimum(field, 0.0)))


def contract(a, b, dims):
    return lax.dot_general(a, b, (dims, ((), ())), preferred_element_type=F32)


def kernel(
    n_seg, n_tp, n_dp, sb,
    tok_hbm, wq_hbm, wk_hbm, wv_hbm, wo_hbm, gate_ref, reset_ref,
    out_hbm,
    tok, w, wo, q, k, v, kf, mem_out, mem_in, read, attn, acc, out,
    tok_sem, w_sem, own_sem, out_sem,
    wy_send, wy_recv, pair_send, dp_send, shard_recv,
    mem_send, mem_recv, at_send, at_recv, fw_send,
):
    seg = lax.axis_index("seg")
    tp = lax.axis_index("tp")
    dp = lax.axis_index("dp")
    ny = n_tp // 2
    y, core = tp // 2, tp % 2
    rows = tok.shape[0]
    groups = q.shape[0]
    blocks = rows // RB
    out_cols = out.shape[1]
    pos = seg % sb
    sibling = y * 2 + (core + 1) % 2

    def tp_peer(dy, dc):
        return ((y + ny - dy) % ny) * 2 + (core + dc) % 2

    def remote(src, dst, send, recv, **where):
        return pltpu.make_async_remote_copy(
            src_ref=src, dst_ref=dst, send_sem=send, recv_sem=recv,
            device_id=where, device_id_type=MESH,
        )

    barrier = pltpu.get_barrier_semaphore()
    for name, size, me in (("tp", n_tp, tp), ("seg", n_seg, seg), ("dp", n_dp, dp)):
        for o in range(1, size):
            pl.semaphore_signal(
                barrier, inc=1, device_id={name: (me + o) % size}, device_id_type=MESH
            )

    def tok_copy(i):
        part = pl.ds(i * MB, MB)
        return pltpu.make_async_copy(tok_hbm.at[part], tok.at[part], tok_sem.at[i])

    def column(kind, g):
        return (3 * g + (2, 0, 1)[kind]) * GW

    def w_copy(kind, g):
        src = (wq_hbm, wk_hbm, wv_hbm)[kind]
        return pltpu.make_async_copy(
            src.at[:, pl.ds(g * GW, GW)], w.at[:, pl.ds(column(kind, g), GW)], w_sem.at[kind, g]
        )

    def own_cols(p):
        return pl.ds(pl.multiple_of(p * out_cols, out_cols), out_cols)

    own_copy = pltpu.make_async_copy(wo_hbm.at[:, :, own_cols(tp)], wo.at[0], own_sem)

    w_copy(1, 0).start()
    w_copy(2, 0).start()
    for i in range(rows // MB):
        tok_copy(i).start()
    w_copy(0, 0).start()
    for g in range(1, groups):
        for kind in (1, 2, 0):
            w_copy(kind, g).start()
    own_copy.start()

    pl.semaphore_wait(barrier, n_tp - 1 + n_seg - 1 + n_dp - 1)

    mine = dp * sb + pos

    def wo_copy(dy, dc):
        slot = 2 * dy + dc
        peer = tp_peer(dy, dc)
        if dy == 0:
            src, dst = wo_hbm.at[:, :, own_cols(peer)], wo.at[slot]
        else:
            src, dst = wo_hbm.at[mine, :, own_cols(peer)], wo.at[slot, mine]
        return remote(src, dst, wy_send.at[slot], wy_recv.at[slot], tp=peer)

    others = [(dy, dc) for dy in range(1, ny) for dc in range(2)]
    for dy, dc in others:
        wo_copy(dy, dc).start()
    wo_copy(0, 1).start()

    pair = dp * sb + (pos + 1) % sb
    partner = seg + 1 - 2 * pos
    half = (n_tp - 2) // 2

    def shard_copy(part, index, send, **where):
        block = wo.at[pl.ds(2 + part * half, half), index]
        return remote(block, block, send, shard_recv.at[part, index], **where)

    def to_pair(part, index, step):
        return shard_copy(part, index, pair_send.at[part, step], seg=partner)

    def to_dp(part, index, step):
        return [
            shard_copy(part, index, dp_send.at[part, step, o], dp=(dp + o) % n_dp)
            for o in range(1, n_dp)
        ]

    def across(o):
        return ((dp + o) % n_dp) * sb + pos

    def own_shard(part):
        for dy, dc in others[part * half : (part + 1) * half]:
            wo_copy(dy, dc).wait_recv()
        to_pair(part, mine, 0).start()
        for copy in to_dp(part, mine, 0):
            copy.start()

    def pass_on(part):
        if part == 0:
            to_pair(0, pair, 0).wait_recv()
            for copy in to_dp(0, pair, 1):
                copy.start()
        else:
            for o in range(1, n_dp):
                to_pair(1, across(o), 0).wait_recv()
                to_pair(1, across(o), o).start()

    def all_shards():
        to_pair(1, pair, 0).wait_recv()
        for o in range(1, n_dp):
            other = ((dp + o) % n_dp) * sb + (pos + 1) % sb
            to_pair(0, across(o), 0).wait_recv()
            to_pair(0, other, 0).wait_recv()
            to_pair(1, other, 0).wait_recv()

    def shards_sent():
        for part in range(2):
            to_pair(part, mine, 0).wait_send()
            for copy in to_dp(part, mine, 0):
                copy.wait_send()
        for copy in to_dp(0, pair, 1):
            copy.wait_send()
        for o in range(1, n_dp):
            to_pair(1, across(o), o).wait_send()

    def mem_copy(g, o):
        return remote(
            mem_out.at[g], mem_in.at[seg, g], mem_send.at[g, o], mem_recv.at[seg, g], seg=seg + o
        )

    def project(parts, first=False, midway=None):
        for kind, g in parts:
            w_copy(kind, g).wait()
        start = column(*parts[0])
        stop = start + len(parts) * GW
        for i in range(rows // MB):
            if first:
                tok_copy(i).wait()
            if midway is not None and i == 1:
                midway()
            part = pl.ds(i * MB, MB)
            wide = contract(tok[part, :], w[:, start:stop], ((1,), (0,))).astype(BF)
            for n, (kind, g) in enumerate(parts):
                val = wide[:, n * GW : (n + 1) * GW]
                (q, k, v)[kind][g, part, :] = val
                if kind == 1:
                    kf[part, :] = features(val.astype(F32)).astype(BF)

    keep = jnp.full((1, DH), 1.0 - reset_ref[0].astype(F32), F32)

    def send_delta(g):
        both = contract(kf[...], v[g], ((0,), (0,)))
        mem_out[g, :DH, :] = both[:DH, :DH].astype(BF)
        mem_out[g, DH:GW, :] = both[DH:, DH:].astype(BF)
        norm = jnp.sum(kf[...].astype(F32), axis=0, keepdims=True)
        row = lax.broadcasted_iota(jnp.int32, (16, DH), 0)
        tail = jnp.where(row == 0, norm[:, :DH], jnp.where(row == 1, norm[:, DH:], 0.0))
        tail = jnp.where(row == 2, keep, tail)
        mem_out[g, GW:, :] = tail.astype(BF)
        for o in range(n_seg - 1, 0, -1):
            @pl.when(seg + o < n_seg)
            def _():
                mem_copy(g, o).start()

    def take_state(g):
        def body(j, state):
            mem, norm = state
            remote(
                mem_out.at[g], mem_in.at[j, g], mem_send.at[g, 0], mem_recv.at[j, g], seg=seg
            ).wait_recv()
            tail = mem_in[j, g, GW:, :].astype(F32)
            held = tail[2:3, :]
            return held * mem + mem_in[j, g, :GW, :].astype(F32), held * norm + tail

        mem, norm = lax.fori_loop(
            0, seg, body, (jnp.zeros((GW, DH), F32), jnp.zeros((16, DH), F32))
        )
        mem = keep * mem
        norm = keep * norm
        row = lax.broadcasted_iota(jnp.int32, (GW, DH), 0)
        read[:, :DH] = jnp.where(row < DH, mem, 0.0).astype(BF)
        read[:, DH:GW] = jnp.where(row < DH, 0.0, mem).astype(BF)
        first = jnp.broadcast_to(norm[0:1, :], (DH, DH)).T.astype(BF)
        second = jnp.broadcast_to(norm[1:2, :], (DH, DH)).T.astype(BF)
        nil = jnp.zeros((DH, DH), BF)
        read[:DH, GW : GW + DH] = first
        read[DH:, GW : GW + DH] = nil
        read[:DH, GW + DH :] = nil
        read[DH:, GW + DH :] = second

    def piece(ref, slot, g, r):
        return ref.at[slot, g, pl.ds(r * RB, RB)]

    def at_copy(dy, g, r):
        slot = 2 * dy if dy else 1
        peer = tp_peer(dy, 0) if dy else sibling
        return remote(
            piece(attn, 0, g, r), piece(attn, slot, g, r),
            at_send.at[dy, g, r], at_recv.at[slot, g, r], tp=peer,
        )

    def fw_copy(dy, g, r):
        return remote(
            piece(attn, 2 * dy, g, r), piece(attn, 2 * dy + 1, g, r),
            fw_send.at[dy, g, r], at_recv.at[2 * dy + 1, g, r], tp=sibling,
        )

    gate_row = jax.nn.sigmoid(
        jnp.concatenate([jnp.full((1, DH), gate_ref[n], F32) for n in range(2 * groups)], axis=1)
    )
    row_at = lax.broadcasted_iota(jnp.int32, (RB, RB), 0)
    col_at = lax.broadcasted_iota(jnp.int32, (RB, RB), 1)

    def attend(g, r):
        part = pl.ds(r * RB, RB)
        query = q[g, part, :]
        qf = features(query.astype(F32)).astype(BF)
        both = contract(qf, read[...], ((1,), (0,)))
        mem_att = both[:, :GW] / jnp.maximum(both[:, GW:], 1.0)
        gate = gate_row[:, g * GW : (g + 1) * GW]
        local = []
        for h in range(2):
            lanes = slice(h * DH, (h + 1) * DH)
            qh = query[:, lanes]
            near = contract(qh, k[g, part, lanes], ((1,), (1,)))
            near = jnp.where(row_at >= col_at, near, -jnp.inf)
            peak = jnp.max(near, axis=-1, keepdims=True)
            if r:
                far = contract(qh, k[g, : r * RB, lanes], ((1,), (1,)))
                peak = jnp.maximum(peak, jnp.max(far, axis=-1, keepdims=True))
            probs = jnp.exp2((near - peak) * SCALE).astype(BF)
            ones = jnp.ones((RB, DH), BF)
            summed = contract(
                probs, jnp.concatenate([v[g, part, lanes], ones], axis=1), ((1,), (0,))
            )
            if r:
                probs = jnp.exp2((far - peak) * SCALE).astype(BF)
                ones = jnp.ones((r * RB, DH), BF)
                summed += contract(
                    probs, jnp.concatenate([v[g, : r * RB, lanes], ones], axis=1), ((1,), (0,))
                )
            local.append(summed[:, :DH] / summed[:, DH:])
        local = jnp.concatenate(local, axis=1)
        attn[0, g, part, :] = (gate * mem_att + (1.0 - gate) * local).astype(BF)
        for dy in range(ny - 1, -1, -1):
            at_copy(dy, g, r).start()

    def wo_rows(slot, g):
        per = GW // wo.shape[2]
        return wo[slot, g * per : (g + 1) * per].reshape(GW, out_cols)

    def near_out(g):
        for r in range(blocks):
            part = pl.ds(r * RB, RB)
            at_copy(0, g, r).wait_recv()
            total = contract(attn[0, g, part, :], wo_rows(0, g), ((1,), (0,)))
            total += contract(attn[1, g, part, :], wo_rows(1, g), ((1,), (0,)))
            if g:
                total += acc[part, :]
            acc[part, :] = total

    project([(1, 0), (2, 0)], first=True)
    send_delta(0)
    project([(0, 0)] + [(1, 1)] * (groups > 1), midway=lambda: own_shard(0))
    own_shard(1)
    for g in range(groups):
        if g:
            project([(2, g)])
            send_delta(g)
            if g == 1:
                pass_on(0)
            project([(0, g)] + [(1, g + 1)] * (g + 1 < groups))
            if g == 1:
                own_copy.wait()
                wo_copy(0, 1).wait_recv()
                pass_on(1)
            near_out(g - 1)
        take_state(g)
        for r in range(blocks):
            attend(g, r)
    if groups == 1:
        own_copy.wait()
        wo_copy(0, 1).wait_recv()
        pass_on(0)
        pass_on(1)
    near_out(groups - 1)
    all_shards()

    def out_copy(r):
        part = pl.ds(r * RB, RB)
        return pltpu.make_async_copy(out.at[part], out_hbm.at[part], out_sem.at[r])

    order = [(g, r) for g in range(groups) for r in range(blocks)]

    def add(slot, g, r):
        part = pl.ds(r * RB, RB)
        acc[part, :] += contract(attn[slot, g, part, :], wo_rows(slot, g), ((1,), (0,)))

    def add_forwarded(g, r):
        for dy in range(1, ny):
            fw_copy(dy, g, r).wait_recv()
            add(2 * dy + 1, g, r)
        if g == groups - 1:
            part = pl.ds(r * RB, RB)
            out[part, :] = acc[part, :].astype(BF)
            out_copy(r).start()

    for n, (g, r) in enumerate(order):
        for dy in range(1, ny):
            at_copy(dy, g, r).wait_recv()
            fw_copy(dy, g, r).start()
            add(2 * dy, g, r)
        if n:
            add_forwarded(*order[n - 1])
    add_forwarded(*order[-1])

    for r in range(blocks):
        out_copy(r).wait()
    for dy, dc in others + [(0, 1)]:
        wo_copy(dy, dc).wait_send()
    shards_sent()
    for g in range(groups):
        for o in range(1, n_seg):
            @pl.when(seg + o < n_seg)
            def _():
                mem_copy(g, o).wait_send()
    for g, r in order:
        for dy in range(ny):
            at_copy(dy, g, r).wait_send()
        for dy in range(1, ny):
            fw_copy(dy, g, r).wait_send()


def on_device(sizes, tokens, w_query, w_key, w_value, w_out, mem_gate, resets):
    n_seg, n_tp, n_dp = sizes
    rows, width = tokens.shape
    depth = w_out.shape[0]
    groups = depth // GW
    out_cols = w_out.shape[1] // n_tp
    blocks = rows // RB
    sb = 2
    shards = n_dp * sb
    dma = pltpu.SemaphoreType.DMA
    hbm = pl.BlockSpec(memory_space=pl.ANY)
    smem = pl.BlockSpec(memory_space=pltpu.SMEM)
    flops = 2 * rows * width * depth * 4 + 4 * rows * rows * depth
    return pl.pallas_call(
        functools.partial(kernel, n_seg, n_tp, n_dp, sb),
        out_shape=jax.ShapeDtypeStruct((rows, out_cols), BF),
        in_specs=[hbm] * 5 + [smem] * 2,
        out_specs=hbm,
        scratch_shapes=[
            pltpu.VMEM((rows, width), BF),
            pltpu.VMEM((width, 3 * groups * GW), BF),
            pltpu.VMEM((n_tp, shards, depth // shards, out_cols), BF),
            pltpu.VMEM((groups, rows, GW), BF),
            pltpu.VMEM((groups, rows, GW), BF),
            pltpu.VMEM((groups, rows, GW), BF),
            pltpu.VMEM((rows, GW), BF),
            pltpu.VMEM((groups, GW + 16, DH), BF),
            pltpu.VMEM((n_seg, groups, GW + 16, DH), BF),
            pltpu.VMEM((GW, 2 * GW), BF),
            pltpu.VMEM((n_tp, groups, rows, GW), BF),
            pltpu.VMEM((rows, out_cols), F32),
            pltpu.VMEM((rows, out_cols), BF),
            dma((rows // MB,)),
            dma((3, groups)),
            dma(()),
            dma((blocks,)),
            dma((n_tp,)),
            dma((n_tp,)),
            dma((2, n_dp)),
            dma((2, 2, n_dp)),
            dma((2, shards)),
            dma((groups, n_seg)),
            dma((n_seg, groups)),
            dma((n_tp // 2, groups, blocks)),
            dma((n_tp, groups, blocks)),
            dma((n_tp // 2, groups, blocks)),
        ],
        compiler_params=pltpu.CompilerParams(
            collective_id=0, has_side_effects=True, vmem_limit_bytes=60 * 1024 * 1024
        ),
        cost_estimate=pl.CostEstimate(
            flops=flops, bytes_accessed=4 * width * depth * 2 + rows * width * 2, transcendentals=0
        ),
    )(tokens, w_query, w_key, w_value, w_out.reshape(shards, depth // shards, width), mem_gate, resets)


def solution(mesh):
    placed = (
        P(("dp", "seg"), None),
        P(None, "tp"),
        P(None, "tp"),
        P(None, "tp"),
        P("tp", None),
        P("tp"),
        P(("dp", "seg")),
    )
    sizes = (mesh.shape["seg"], mesh.shape["tp"], mesh.shape["dp"])
    return jax.shard_map(
        functools.partial(on_device, sizes),
        mesh=mesh, in_specs=placed, out_specs=P(("dp", "seg"), "tp"), check_vma=False,
    )
```
